256 devices in a mesh: mode: 16 (over y, z_hi), elem: 16 (over x, z_lo, core).
Axes of the slice: x: 4, y: 4, z: 8 (z_hi: 4, z_lo: 2; z = z_hi * 2 + z_lo), core: 2. Of those that a mesh axis runs over, the one named last changes fastest.
Arguments:
- velocity: bfloat16 [2, 2, 512, 81, 2048], P(None, None, 'mode', None, 'elem'), may hold values from -0.119628906 to 0.119628906
- concentration: bfloat16 [1024, 81, 2048], P(None, None, ('elem', 'mode')), may hold values from 0.049804688 to 0.546875
- stiffness: bfloat16 [4, 81, 81], replicated, may hold values from -0.625 to 0.625
- block_ids: int32 [2048], P('elem'), may hold values from 0 to 3
- radial_weight: float32 [81, 2048], P(None, 'elem'), may hold values from 0.5 to 4
Outputs:
- operator_image: float32 [2, 2, 512, 81, 2048], P(None, None, 'mode', None, 'elem')
The draws below stay inside these ranges and needn't reach their ends.
All inputs are finite; a program needn't handle non-finite values.
Results may differ from the reference program's by a relative error of at most 0.0051.
Values may be sent and summed in bfloat16 or wider, within the bound.
No kernel may reach another device: no remote copies, remote signals or barrier semaphores. Data moves between devices by JAX's collectives and lax.ppermute only.
A program may use at most 128 MiB of HBM per device.

```python
import math
import jax
import jax.numpy as jnp
from jax import lax

MODES = 512
NPHI = 1024
NODE = 81
NTYPE = 4
EZ = 16
E_DEV = 128
ELEMS = 2048


def set_ends(result, key, low, largest):
    place = [jax.random.randint(jax.random.fold_in(key, axis), (), 0, length) for axis, length in enumerate(result.shape)]
    main_axis = result.shape.index(max(result.shape))
    next_to = place[:main_axis] + [(place[main_axis] + 1) % result.shape[main_axis]] + place[main_axis + 1:]
    return result.at[tuple(place)].set(low).at[tuple(next_to)].set(largest)


def level_of(rng, extent, cuts, low, top_value):
    def one(position, blocks):
        steps = jax.random.uniform(jax.random.fold_in(jax.random.fold_in(rng, 6), position), (blocks,), jnp.float32, low / len(cuts), top_value / len(cuts))
        return jnp.repeat(jnp.exp(steps), extent[position] // blocks).reshape((-1,) + (1,) * (len(extent) - position - 1))

    gain = one(*cuts[0])
    for cut in cuts[1:]:
        gain = gain * one(*cut)
    return gain


def centred(stream_key, dims, deviation, limit, pieces=(), kind=jnp.bfloat16):
    drawn = deviation * jax.random.normal(stream_key, dims, jnp.float32)
    if pieces:
        drawn = drawn * level_of(stream_key, dims, pieces, -0.22, 0.18)
    return jnp.clip(drawn, -limit, limit).astype(kind)


def setup_inputs(seed: int = 0) -> dict:
    seeds = jax.random.split(jax.random.key(seed), 6)
    return {
        "velocity": centred(seeds[0], (2, 2, MODES, NODE, ELEMS), 0.02, 0.119628906, ((2, 16), (4, 16))),
        "concentration": jnp.clip(0.049804688 + 0.4970703 * jax.random.uniform(seeds[1], (NPHI, NODE, ELEMS), jnp.float32) ** level_of(seeds[1], (NPHI, NODE, ELEMS), ((2, 256),), -0.2, 0.2), 0.049804688, 0.546875).astype(jnp.bfloat16),
        "stiffness": centred(seeds[2], (NTYPE, NODE, NODE), NODE ** -0.5, 0.625),
        "block_ids": set_ends(jax.random.randint(seeds[3], (ELEMS,), 0, NTYPE), jax.random.fold_in(seeds[3], 1), 0, NTYPE - 1).astype(jnp.int32),
        "radial_weight": jnp.clip(jnp.exp(math.log(4.0) - 2.0794415 * jax.random.uniform(seeds[4], (NODE, ELEMS), jnp.float32) ** level_of(seeds[4], (NODE, ELEMS), ((1, 16),), -0.2, 0.2)), 0.5, 4.0),
    }


packing_limit = 0.68
krieger_power = 1.82


def azimuth_tables():
    planes = jnp.arange(NPHI, dtype=jnp.int32)
    orders = jnp.arange(MODES, dtype=jnp.int32)
    phase = (planes[:, None] * orders[None, :]) % NPHI
    angle = (2.0 * jnp.pi / NPHI) * phase.astype(jnp.float32)
    weight = jnp.where(orders == 0, 1.0, 2.0).astype(jnp.float32)
    cosine = jnp.cos(angle)
    sine = jnp.sin(angle)
    inverse = jnp.concatenate([weight * cosine, -weight * sine], axis=1).astype(jnp.bfloat16)
    forward = (jnp.concatenate([cosine.T, -sine.T], axis=0) / NPHI).astype(jnp.bfloat16)
    return inverse, forward


def viscosity_of(conc):
    return (1.0 - conc.astype(jnp.float32) / packing_limit) ** (-krieger_power)


def helmholtz_apply(field, ids, weight, stiffness, scale):
    total = (4.0 * scale[:, None, None] ** 2 * weight[None]) * field
    for block_type in range(NTYPE):
        mask = (ids == block_type).astype(jnp.float32)
        coupled = jnp.einsum('ij,crmjb->crmib', stiffness[block_type].astype(jnp.float32), field,
                             precision=lax.Precision.HIGHEST)
        total = total + mask * coupled
    return total


def assemble_axial(image):
    upper = image[:, :, :, :, 8]
    lower = image[:, :, :, :, 0]
    pad_high = ((0, 0),) * 5 + ((0, 1),)
    pad_low = ((0, 0),) * 5 + ((1, 0),)
    new_upper = upper + jnp.pad(lower[..., 1:], pad_high)
    new_lower = lower + jnp.pad(upper[..., :-1], pad_low)
    return image.at[:, :, :, :, 8].set(new_upper).at[:, :, :, :, 0].set(new_lower)


def assemble_radial(image):
    outer = image[:, :, :, 8]
    inner = image[:, :, :, 0]
    pad_high = ((0, 0),) * 4 + ((0, 1), (0, 0))
    pad_low = ((0, 0),) * 4 + ((1, 0), (0, 0))
    new_outer = outer + jnp.pad(inner[:, :, :, :, 1:], pad_high)
    new_inner = inner + jnp.pad(outer[:, :, :, :, :-1], pad_low)
    return image.at[:, :, :, 8].set(new_outer).at[:, :, :, 0].set(new_inner)


def reference(velocity, concentration, stiffness, block_ids, radial_weight):
    inverse, forward = azimuth_tables()
    inverse_wide = inverse.astype(jnp.float32)
    forward_wide = forward.astype(jnp.float32)
    scale = jnp.arange(MODES, dtype=jnp.int32).astype(jnp.float32) / MODES
    blocks = ELEMS // E_DEV

    def one_block(items):
        speed, conc, ids, weight = items
        flat_modes = speed.astype(jnp.float32).reshape(2, 2 * MODES, NODE * E_DEV)
        physical = jnp.einsum('pk,ckn->cpn', inverse_wide, flat_modes, precision=lax.Precision.HIGHEST)
        product = (viscosity_of(conc.reshape(NPHI, NODE * E_DEV))[None] * physical).astype(jnp.bfloat16)
        spectral = jnp.einsum('kp,cpn->ckn', forward_wide, product.astype(jnp.float32),
                              precision=lax.Precision.HIGHEST).astype(jnp.bfloat16)
        spectral = spectral.reshape(2, 2, MODES, NODE, E_DEV).astype(jnp.float32)
        return helmholtz_apply(spectral, ids, weight, stiffness, scale)

    speed_blocks = jnp.moveaxis(velocity.reshape(2, 2, MODES, NODE, blocks, E_DEV), 4, 0)
    conc_blocks = jnp.moveaxis(concentration.reshape(NPHI, NODE, blocks, E_DEV), 2, 0)
    id_blocks = block_ids.reshape(blocks, E_DEV)
    weight_blocks = jnp.moveaxis(radial_weight.reshape(NODE, blocks, E_DEV), 1, 0)
    images = lax.map(one_block, (speed_blocks, conc_blocks, id_blocks, weight_blocks))
    image = jnp.moveaxis(images, 0, 4).reshape(2, 2, MODES, 9, 9, ELEMS // EZ, EZ)
    image = assemble_axial(image)
    image = assemble_radial(image)
    return image.reshape(2, 2, MODES, NODE, ELEMS)
```

```python
import functools

import jax
import jax.numpy as jnp
from jax import lax
from jax.experimental import pallas as pl
from jax.experimental.pallas import tpu as pltpu
from jax.sharding import PartitionSpec as P

MODES = 512
NPHI = 1024
NODE = 81
EZ = 16
LANES = 128
VMEM_BYTES = 56 * 1024 * 1024

packing_limit = 0.68
krieger_power = 1.82


def params(*semantics):
    return pltpu.CompilerParams(
        vmem_limit_bytes=VMEM_BYTES, dimension_semantics=semantics or None
    )


def azimuth_tables(groups):
    planes = jnp.arange(NPHI, dtype=jnp.int32)
    orders = jnp.arange(MODES, dtype=jnp.int32)
    phase = planes[:, None] * orders[None, :] % NPHI
    angle = 2.0 * jnp.pi / NPHI * phase.astype(jnp.float32)
    weight = jnp.where(orders == 0, 1.0, 2.0).astype(jnp.float32)
    cosine = jnp.cos(angle)
    sine = jnp.sin(angle)
    inverse = jnp.stack(
        [
            (weight * cosine).T.astype(jnp.bfloat16).reshape(groups, -1, NPHI),
            (-weight * sine).T.astype(jnp.bfloat16).reshape(groups, -1, NPHI),
        ],
        axis=1,
    ).reshape(2 * MODES, NPHI)
    forward = jnp.stack(
        [
            (cosine / NPHI).astype(jnp.bfloat16).reshape(NPHI, groups, -1),
            (-sine / NPHI).astype(jnp.bfloat16).reshape(NPHI, groups, -1),
        ],
        axis=2,
    ).reshape(NPHI, 2 * MODES)
    return inverse, forward


def pack_kernel(v_ref, o_ref):
    nodes = v_ref.shape[2]
    for k in range(nodes):
        tile = v_ref[:, :, k].reshape(LANES, LANES)
        o_ref[:, k] = tile.T.reshape(o_ref.shape[0], -1, LANES)


def pack(velocity, groups, piece):
    step = 9
    modes = velocity.shape[3]
    return pl.pallas_call(
        pack_kernel,
        grid=(NODE // step,),
        in_specs=[
            pl.BlockSpec((2, 2, step, modes, LANES), lambda i: (0, 0, i, 0, 0))
        ],
        out_specs=pl.BlockSpec((groups, step, piece, LANES), lambda i: (0, i, 0, 0)),
        out_shape=jax.ShapeDtypeStruct((groups, NODE, piece, LANES), jnp.bfloat16),
        compiler_params=params("arbitrary"),
        name="pack_by_element_group",
    )(velocity)


def swap_halves(even, odd, low):
    half = LANES // 2
    return (
        jnp.where(low, even, pltpu.roll(odd, half, 1)),
        jnp.where(low, pltpu.roll(even, half, 1), odd),
    )


def azimuth_kernel(x_ref, inv_ref, fwd_ref, visc_ref, couple_ref, weight_ref, o_ref,
                   field_ref, image_ref):
    groups, rows, _ = x_ref.shape
    lane = lax.broadcasted_iota(jnp.int32, (rows, LANES), 1)
    low = lane < LANES // 2
    for t in range(groups // 2):
        first, second = swap_halves(
            x_ref[2 * t].astype(jnp.float32), x_ref[2 * t + 1].astype(jnp.float32), low
        )
        field_ref[0, :, t * LANES:(t + 1) * LANES] = first.astype(jnp.bfloat16)
        field_ref[1, :, t * LANES:(t + 1) * LANES] = second.astype(jnp.bfloat16)
    for c in range(2):
        physical = jnp.dot(field_ref[c], inv_ref[...], preferred_element_type=jnp.float32)
        product = (visc_ref[...] * physical).astype(jnp.bfloat16)
        spectral = jnp.dot(
            product, fwd_ref[...], preferred_element_type=jnp.float32
        ).astype(jnp.bfloat16)
        column = lax.broadcasted_iota(jnp.int32, (1, 2 * MODES), 1)
        order = (column // 64) * 32 + column % 32
        scale = 4.0 * (order.astype(jnp.float32) / MODES) ** 2
        image_ref[c] = jnp.dot(
            couple_ref[...], spectral, preferred_element_type=jnp.float32
        ) + (weight_ref[...] * scale) * spectral.astype(jnp.float32)
    for t in range(groups // 2):
        first, second = swap_halves(
            image_ref[0, :, t * LANES:(t + 1) * LANES],
            image_ref[1, :, t * LANES:(t + 1) * LANES],
            low,
        )
        o_ref[2 * t] = first.astype(jnp.bfloat16)
        o_ref[2 * t + 1] = second.astype(jnp.bfloat16)


def azimuth(gathered, inverse, forward, viscosity, coupling, weight):
    groups, rows, _ = gathered.shape
    return pl.pallas_call(
        azimuth_kernel,
        out_shape=jax.ShapeDtypeStruct(gathered.shape, jnp.bfloat16),
        scratch_shapes=[
            pltpu.VMEM((2, rows, 2 * MODES), jnp.bfloat16),
            pltpu.VMEM((2, rows, 2 * MODES), jnp.float32),
        ],
        compiler_params=params(),
        name="azimuth_product_and_coupling",
    )(gathered, inverse, forward, viscosity, coupling, weight)


def write_nodes(o_ref, tiles):
    lane = lax.broadcasted_iota(jnp.int32, (LANES, LANES), 1)
    place = lane % EZ
    first, last = tiles[0], tiles[8]
    tiles = list(tiles)
    tiles[8] = last + jnp.where(place < EZ - 1, pltpu.roll(first, LANES - 1, 1), 0.0)
    tiles[0] = first + jnp.where(place > 0, pltpu.roll(last, 1, 1), 0.0)
    for b in range(9):
        o_ref[:, :, b] = tiles[b].reshape(2, 2, -1, LANES)


def interior_kernel(z_ref, o_ref):
    tiles = []
    for b in range(9):
        tiles.append(z_ref[:, b].astype(jnp.float32).reshape(LANES, LANES).T)
    write_nodes(o_ref, tiles)


def face_kernel(inner_ref, outer_ref, prev_ref, next_ref, kept_ref, o_ref):
    tail = prev_ref.shape[0]

    def face(own_ref, b, before, after):
        own = own_ref[:, b].astype(jnp.float32)
        other = jnp.concatenate([before, after], axis=0).astype(jnp.float32)
        return (own + other).reshape(LANES, LANES).T

    @pl.when(pl.program_id(0) == 0)
    def _():
        write_nodes(
            o_ref,
            [face(inner_ref, b, prev_ref[:, b], outer_ref[:-tail, b]) for b in range(9)],
        )

    @pl.when(pl.program_id(0) == 1)
    def _():
        write_nodes(
            o_ref,
            [face(outer_ref, b, inner_ref[tail:, b], next_ref[:, b]) for b in range(9)],
        )


def assemble(returned, modes):
    groups, _, piece, _ = returned.shape
    faces = EZ // piece
    count = lax.axis_size("elem")
    from_next = lax.ppermute(
        returned[:faces, :9], "elem", [(e, e - 1) for e in range(1, count)]
    )
    from_prev = lax.ppermute(
        returned[-faces:, 72:], "elem", [(e, e + 1) for e in range(count - 1)]
    )
    out = jax.ShapeDtypeStruct((2, 2, NODE, modes, LANES), jnp.float32)
    block = (groups, 9, piece, LANES)
    image_block = (2, 2, 9, modes, LANES)
    image = pl.pallas_call(
        interior_kernel,
        grid=(7,),
        in_specs=[pl.BlockSpec(block, lambda i: (0, i + 1, 0, 0))],
        out_specs=pl.BlockSpec(image_block, lambda i: (0, 0, i + 1, 0, 0)),
        out_shape=out,
        compiler_params=params("arbitrary"),
        name="interior_nodes",
    )(returned)
    face_block = pl.BlockSpec((faces, 9, piece, LANES), lambda i: (0, 0, 0, 0))
    return pl.pallas_call(
        face_kernel,
        grid=(2,),
        in_specs=[
            pl.BlockSpec(block, lambda i: (0, 0, 0, 0)),
            pl.BlockSpec(block, lambda i: (0, 8, 0, 0)),
            face_block,
            face_block,
            pl.BlockSpec(memory_space=pl.ANY),
        ],
        out_specs=pl.BlockSpec(image_block, lambda i: (0, 0, 8 * i, 0, 0)),
        out_shape=out,
        input_output_aliases={4: 0},
        compiler_params=params("arbitrary"),
        name="radial_face_nodes",
    )(returned, returned, from_prev, from_next, image)


def body(velocity, concentration, stiffness, block_ids, radial_weight):
    modes = velocity.shape[2]
    elements = velocity.shape[4]
    groups = lax.axis_size("mode")
    piece = elements // groups
    rows = NODE * piece
    packed = pack(velocity.transpose(0, 1, 3, 2, 4), groups, piece)
    gathered = lax.all_to_all(
        packed.reshape(groups, rows, LANES), "mode", split_axis=0, concat_axis=0, tiled=True
    )

    inverse, forward = azimuth_tables(groups)
    viscosity = (
        1.0
        - concentration.transpose(1, 2, 0).reshape(rows, NPHI).astype(jnp.float32)
        / packing_limit
    ) ** (-krieger_power)
    first = lax.axis_index("mode") * piece
    ids = lax.dynamic_slice(block_ids, (first,), (piece,))
    weight = lax.dynamic_slice(radial_weight, (0, first), (NODE, piece)).reshape(rows, 1)
    chosen = sum(
        jnp.where((ids == kind)[None, :, None], stiffness[kind][:, None, :], 0)
        for kind in range(stiffness.shape[0])
    )
    same = jnp.eye(piece, dtype=jnp.bool_)
    coupling = jnp.where(
        same[None, :, None, :], chosen[:, :, :, None], jnp.bfloat16(0)
    ).reshape(rows, rows)

    images = azimuth(gathered, inverse, forward, viscosity, coupling, weight)
    returned = lax.all_to_all(images, "mode", split_axis=0, concat_axis=0, tiled=True)
    image = assemble(returned.reshape(groups, NODE, piece, LANES), modes)
    return image.transpose(0, 1, 3, 2, 4)


def solution(mesh):
    in_specs = (
        P(None, None, "mode", None, "elem"),
        P(None, None, ("elem", "mode")),
        P(),
        P("elem"),
        P(None, "elem"),
    )
    out_specs = P(None, None, "mode", None, "elem")
    return jax.shard_map(body, mesh=mesh, in_specs=in_specs, out_specs=out_specs, check_vma=False)
```

```python
import functools

import jax
import jax.numpy as jnp
from jax import lax
from jax.experimental import pallas as pl
from jax.experimental.pallas import tpu as pltpu
from jax.sharding import PartitionSpec as P

MODES = 512
NPHI = 1024
NODE = 81
EZ = 16
LANES = 128
FACE = 9
EXTRA = 16

packing_limit = 0.68
krieger_power = 1.82


def params(mebibytes, *semantics):
    return pltpu.CompilerParams(
        vmem_limit_bytes=mebibytes * 1024 * 1024, dimension_semantics=semantics or None
    )


def azimuth_tables(groups):
    planes = jnp.arange(NPHI, dtype=jnp.int32)
    orders = jnp.arange(MODES, dtype=jnp.int32)
    phase = orders[:, None] * planes[None, :] % NPHI
    angle = 2.0 * jnp.pi / NPHI * phase.astype(jnp.float32)
    shape = (groups, MODES // groups, NPHI)
    base = jnp.stack(
        [
            jnp.cos(angle).astype(jnp.bfloat16).reshape(shape),
            (-jnp.sin(angle)).astype(jnp.bfloat16).reshape(shape),
        ],
        axis=1,
    ).reshape(2 * MODES, NPHI)
    base = lax.optimization_barrier(base)
    column = jnp.arange(2 * MODES, dtype=jnp.int32)
    weight = jnp.where(column % 32 + column // 64 == 0, 1, 2)
    inverse = base * weight.astype(jnp.bfloat16)[:, None]
    forward = base.T / jnp.bfloat16(NPHI)
    return inverse, forward


def pack_kernel(v_ref, o_ref):
    nodes = v_ref.shape[2]
    for k in range(nodes):
        tile = v_ref[:, :, k].reshape(LANES, LANES)
        o_ref[:, k] = tile.T.reshape(o_ref.shape[0], -1, LANES)


def pack(velocity, groups, piece):
    step = 27
    modes = velocity.shape[3]
    return pl.pallas_call(
        pack_kernel,
        grid=(NODE // step,),
        in_specs=[
            pl.BlockSpec((2, 2, step, modes, LANES), lambda i: (0, 0, i, 0, 0))
        ],
        out_specs=pl.BlockSpec((groups, step, piece, LANES), lambda i: (0, i, 0, 0)),
        out_shape=jax.ShapeDtypeStruct((groups, NODE, piece, LANES), jnp.bfloat16),
        compiler_params=params(58, "arbitrary"),
        name="pack_by_element_group",
    )(velocity)


def swap_halves(even, odd, low):
    half = LANES // 2
    return (
        jnp.where(low, even, pltpu.roll(odd, half, 1)),
        jnp.where(low, pltpu.roll(even, half, 1), odd),
    )


def azimuth_kernel(x_ref, inv_hbm, visc_hbm, fwd_hbm, couple_hbm, weight_ref, o_ref,
                   inv_ref, visc_ref, fwd_ref, couple_ref, field_ref, image_ref, sems):
    groups, rows, _ = x_ref.shape
    pairs = (
        (inv_hbm, inv_ref), (visc_hbm, visc_ref), (fwd_hbm, fwd_ref), (couple_hbm, couple_ref),
    )
    copies = [
        pltpu.make_async_copy(source, target, sems.at[k])
        for k, (source, target) in enumerate(pairs)
    ]
    for copy in copies:
        copy.start()
    lane = lax.broadcasted_iota(jnp.int32, (rows, LANES), 1)
    low = lane < LANES // 2
    for t in range(groups // 2):
        first, second = swap_halves(
            x_ref[2 * t].astype(jnp.float32), x_ref[2 * t + 1].astype(jnp.float32), low
        )
        field_ref[0, :, t * LANES:(t + 1) * LANES] = first.astype(jnp.bfloat16)
        field_ref[1, :, t * LANES:(t + 1) * LANES] = second.astype(jnp.bfloat16)
    for c in range(2):
        if c == 0:
            copies[0].wait()
        physical = jnp.dot(field_ref[c], inv_ref[...], preferred_element_type=jnp.float32)
        if c == 0:
            copies[1].wait()
        product = (visc_ref[...] * physical).astype(jnp.bfloat16)
        if c == 0:
            copies[2].wait()
        spectral = jnp.dot(
            product, fwd_ref[...], preferred_element_type=jnp.float32
        ).astype(jnp.bfloat16)
        column = lax.broadcasted_iota(jnp.int32, (1, 2 * MODES), 1)
        order = (column // 64) * 32 + column % 32
        scale = 4.0 * (order.astype(jnp.float32) / MODES) ** 2
        if c == 0:
            copies[3].wait()
        image_ref[c] = jnp.dot(
            couple_ref[...], spectral, preferred_element_type=jnp.float32
        ) + (weight_ref[...] * scale) * spectral.astype(jnp.float32)
    for t in range(groups // 2):
        pair = swap_halves(
            image_ref[0, :, t * LANES:(t + 1) * LANES],
            image_ref[1, :, t * LANES:(t + 1) * LANES],
            low,
        )
        for half in range(2):
            merge_axial(o_ref.at[2 * t + half], pair[half], rows // NODE)


def merge_axial(o_ref, image, piece):
    place = lax.broadcasted_iota(jnp.int32, (piece, LANES), 0)
    lowest = []
    for a in range(FACE):
        start = a * FACE * piece
        inner = image[start:start + piece]
        outer = image[start + 8 * piece:start + 9 * piece]
        outer = outer + jnp.where(place < piece - 1, pltpu.roll(inner, piece - 1, 0), 0.0)
        kept = image[start + piece:start + 8 * piece]
        o_ref[a * 8 * piece:(a + 1) * 8 * piece] = jnp.concatenate(
            [kept, outer], axis=0
        ).astype(jnp.bfloat16)
        lowest.append(inner[:1])
    lowest.append(jnp.zeros((EXTRA - FACE, LANES), jnp.float32))
    o_ref[FACE * 8 * piece:] = jnp.concatenate(lowest, axis=0).astype(jnp.bfloat16)


def azimuth(gathered, inverse, viscosity, forward, coupling, weight):
    groups, rows, _ = gathered.shape
    sent = FACE * 8 * (rows // NODE) + EXTRA
    vmem = pl.BlockSpec(memory_space=pltpu.VMEM)
    hbm = pl.BlockSpec(memory_space=pltpu.HBM)
    held = [
        pltpu.with_memory_space_constraint(value, pltpu.HBM)
        for value in (inverse, viscosity, forward, coupling)
    ]
    return pl.pallas_call(
        azimuth_kernel,
        in_specs=[vmem, hbm, hbm, hbm, hbm, vmem],
        out_specs=vmem,
        out_shape=jax.ShapeDtypeStruct((groups, sent, LANES), jnp.bfloat16),
        scratch_shapes=[pltpu.VMEM(value.shape, value.dtype) for value in held] + [
            pltpu.VMEM((2, rows, 2 * MODES), jnp.bfloat16),
            pltpu.VMEM((2, rows, 2 * MODES), jnp.float32),
            pltpu.SemaphoreType.DMA((len(held),)),
        ],
        compiler_params=params(40),
        name="azimuth_product_and_coupling",
    )(gathered, *held, weight)


def lowest_nodes(values):
    groups = values.shape[0]
    return jnp.broadcast_to(
        values[:, None, :], (groups, LANES // groups, LANES)
    ).reshape(LANES, LANES)


def row_of(extra, a):
    place = lax.broadcasted_iota(jnp.int32, extra.shape, 1)
    return jnp.sum(jnp.where(place == a, extra, 0.0), axis=1)


def write_nodes(o_ref, image, lowest):
    groups, rows, _ = image.shape
    piece = rows // 8
    place = lax.broadcasted_iota(jnp.int32, (LANES, LANES), 1) % EZ
    zero = lowest_nodes(lowest).T
    tiles = []
    for b in range(8):
        tiles.append(image[:, b * piece:(b + 1) * piece].reshape(LANES, LANES).T)
    crossing = (place % piece == piece - 1) & (place < EZ - 1)
    tiles[7] = tiles[7] + jnp.where(crossing, pltpu.roll(zero, LANES - 1, 1), 0.0)
    tiles.insert(0, jnp.where(place == 0, zero, pltpu.roll(tiles[7], 1, 1)))
    for b in range(FACE):
        o_ref[:, :, b] = tiles[b].reshape(2, 2, -1, LANES)


def interior_kernel(z_ref, extra_ref, o_ref):
    a = pl.program_id(0) + 1
    write_nodes(
        o_ref,
        z_ref[...].astype(jnp.float32),
        row_of(extra_ref[...].astype(jnp.float32), a),
    )


def face_kernel(inner_ref, outer_ref, extra_ref, prev_ref, next_ref, kept_ref, o_ref):
    tail = prev_ref.shape[0]
    rows = inner_ref.shape[1]
    wide = lambda value: value.astype(jnp.float32)
    extra = wide(extra_ref[...])

    @pl.when(pl.program_id(0) == 0)
    def _():
        far = wide(prev_ref[...])
        other = jnp.concatenate([far[:, :rows], wide(outer_ref[:-tail])], axis=0)
        ends = jnp.concatenate([row_of(far[:, rows:], 8), row_of(extra[:-tail], 8)], axis=0)
        write_nodes(o_ref, wide(inner_ref[...]) + other, row_of(extra, 0) + ends)

    @pl.when(pl.program_id(0) == 1)
    def _():
        far = wide(next_ref[...])
        other = jnp.concatenate([wide(inner_ref[tail:]), far[:, :rows]], axis=0)
        ends = jnp.concatenate([row_of(extra[tail:], 0), row_of(far[:, rows:], 0)], axis=0)
        write_nodes(o_ref, wide(outer_ref[...]) + other, row_of(extra, 8) + ends)


def assemble(returned, modes, piece):
    groups = returned.shape[0]
    rows = 8 * piece
    faces = EZ // piece
    count = lax.axis_size("elem")
    inner = jnp.concatenate([returned[:faces, :rows], returned[:faces, -EXTRA:]], axis=1)
    outer = jnp.concatenate(
        [returned[-faces:, 8 * rows:9 * rows], returned[-faces:, -EXTRA:]], axis=1
    )
    from_next = lax.ppermute(inner, "elem", [(e, e - 1) for e in range(1, count)])
    from_prev = lax.ppermute(outer, "elem", [(e, e + 1) for e in range(count - 1)])
    out = jax.ShapeDtypeStruct((2, 2, NODE, modes, LANES), jnp.float32)
    block = (groups, rows, LANES)
    extra_block = pl.BlockSpec(
        (groups, EXTRA, LANES), lambda i: (0, FACE * rows // EXTRA, 0)
    )
    image_block = (2, 2, FACE, modes, LANES)
    image = pl.pallas_call(
        interior_kernel,
        grid=(7,),
        in_specs=[pl.BlockSpec(block, lambda i: (0, i + 1, 0)), extra_block],
        out_specs=pl.BlockSpec(image_block, lambda i: (0, 0, i + 1, 0, 0)),
        out_shape=out,
        compiler_params=params(12, "arbitrary"),
        name="interior_nodes",
    )(returned, returned)
    face_block = pl.BlockSpec(from_prev.shape, lambda i: (0, 0, 0))
    return pl.pallas_call(
        face_kernel,
        grid=(2,),
        in_specs=[
            pl.BlockSpec(block, lambda i: (0, 0, 0)),
            pl.BlockSpec(block, lambda i: (0, 8, 0)),
            extra_block,
            face_block,
            face_block,
            pl.BlockSpec(memory_space=pl.ANY),
        ],
        out_specs=pl.BlockSpec(image_block, lambda i: (0, 0, 8 * i, 0, 0)),
        out_shape=out,
        input_output_aliases={5: 0},
        compiler_params=params(12, "arbitrary"),
        name="radial_face_nodes",
    )(returned, returned, returned, from_prev, from_next, image)


def body(velocity, concentration, stiffness, block_ids, radial_weight):
    modes = velocity.shape[2]
    elements = velocity.shape[4]
    groups = lax.axis_size("mode")
    piece = elements // groups
    rows = NODE * piece
    packed = pack(velocity.transpose(0, 1, 3, 2, 4), groups, piece)
    gathered = lax.all_to_all(
        packed.reshape(groups, rows, LANES), "mode", split_axis=0, concat_axis=0, tiled=True
    )

    inverse, forward = azimuth_tables(groups)
    viscosity = (
        1.0
        - concentration.transpose(1, 2, 0).reshape(rows, NPHI).astype(jnp.float32)
        / packing_limit
    ) ** (-krieger_power)
    first = lax.axis_index("mode") * piece
    ids = lax.dynamic_slice(block_ids, (first,), (piece,))
    weight = lax.dynamic_slice(radial_weight, (0, first), (NODE, piece)).reshape(rows, 1)
    row = jnp.arange(rows, dtype=jnp.int32)
    spread = (row[:, None] // piece == jnp.arange(NODE)[None, :]).astype(jnp.bfloat16)
    ids = jnp.tile(ids, NODE)
    kinds = jnp.einsum("ni,tij->tnj", spread, stiffness, preferred_element_type=jnp.bfloat16)
    chosen = jnp.zeros((rows, NODE), jnp.bfloat16)
    for kind in range(stiffness.shape[0]):
        chosen = jnp.where((ids == kind)[:, None], kinds[kind], chosen)
    coupling = jnp.where(
        row[:, None] % piece == row[None, :] % piece,
        jnp.einsum("nj,mj->nm", chosen, spread, preferred_element_type=jnp.bfloat16),
        jnp.bfloat16(0),
    )

    images = azimuth(gathered, inverse, viscosity, forward, coupling, weight)
    returned = lax.all_to_all(images, "mode", split_axis=0, concat_axis=0, tiled=True)
    image = assemble(returned, modes, piece)
    return image.transpose(0, 1, 3, 2, 4)


def solution(mesh):
    in_specs = (
        P(None, None, "mode", None, "elem"),
        P(None, None, ("elem", "mode")),
        P(),
        P("elem"),
        P(None, "elem"),
    )
    out_specs = P(None, None, "mode", None, "elem")
    return jax.shard_map(body, mesh=mesh, in_specs=in_specs, out_specs=out_specs, check_vma=False)
```

```python
import functools

import jax
import jax.numpy as jnp
from jax import lax
from jax.experimental import pallas as pl
from jax.experimental.pallas import tpu as pltpu
from jax.sharding import PartitionSpec as P

MODES = 512
NPHI = 1024
NODE = 81
EZ = 16
LANES = 128
FACE = 9
EXTRA = 16
STAGES = (3, 5, 7)

packing_limit = 0.68
krieger_power = 1.82


def params(mebibytes, *semantics):
    return pltpu.CompilerParams(
        vmem_limit_bytes=mebibytes * 1024 * 1024, dimension_semantics=semantics or None
    )


def azimuth_tables(groups):
    planes = jnp.arange(NPHI, dtype=jnp.int32)
    orders = jnp.arange(MODES, dtype=jnp.int32)
    phase = orders[:, None] * planes[None, :] % NPHI
    angle = 2.0 * jnp.pi / NPHI * phase.astype(jnp.float32)
    shape = (groups, MODES // groups, NPHI)
    base = jnp.stack(
        [
            jnp.cos(angle).astype(jnp.bfloat16).reshape(shape),
            (-jnp.sin(angle)).astype(jnp.bfloat16).reshape(shape),
        ],
        axis=1,
    ).reshape(2 * MODES, NPHI)
    base = lax.optimization_barrier(base)
    column = jnp.arange(2 * MODES, dtype=jnp.int32)
    weight = jnp.where(column % 32 + column // 64 == 0, 1, 2)
    inverse = base * weight.astype(jnp.bfloat16)[:, None]
    forward = base.T / jnp.bfloat16(NPHI)
    return inverse, forward


PACK_STEP = 9


def pack_kernel(v_hbm, o_hbm, v_ref, o_ref, v_sems, o_sems):
    steps = NODE // PACK_STEP
    nodes = [pl.ds(i * PACK_STEP, PACK_STEP) for i in range(steps)]
    arrivals = [
        pltpu.make_async_copy(v_hbm.at[:, :, nodes[i]], v_ref.at[:, :, nodes[i]], v_sems.at[i])
        for i in range(steps)
    ]
    departures = [
        pltpu.make_async_copy(o_ref.at[:, nodes[i]], o_hbm.at[:, nodes[i]], o_sems.at[i])
        for i in range(steps)
    ]
    for copy in arrivals:
        copy.start()
    for i in range(steps):
        arrivals[i].wait()
        for k in range(i * PACK_STEP, (i + 1) * PACK_STEP):
            tile = v_ref[:, :, k].reshape(LANES, LANES)
            o_ref[:, k] = tile.T.reshape(o_ref.shape[0], -1, LANES)
        departures[i].start()
    for copy in departures:
        copy.wait()


def pack(velocity, groups, piece):
    steps = NODE // PACK_STEP
    hbm = pl.BlockSpec(memory_space=pltpu.HBM)
    packed = (groups, NODE, piece, LANES)
    return pl.pallas_call(
        pack_kernel,
        in_specs=[hbm],
        out_specs=hbm,
        out_shape=jax.ShapeDtypeStruct(packed, jnp.bfloat16),
        scratch_shapes=[
            pltpu.VMEM(velocity.shape, jnp.bfloat16),
            pltpu.VMEM(packed, jnp.bfloat16),
            pltpu.SemaphoreType.DMA((steps,)),
            pltpu.SemaphoreType.DMA((steps,)),
        ],
        compiler_params=params(58),
        name="pack_by_element_group",
    )(pltpu.with_memory_space_constraint(velocity, pltpu.HBM))


def swap_halves(even, odd, low):
    half = LANES // 2
    return (
        jnp.where(low, even, pltpu.roll(odd, half, 1)),
        jnp.where(low, pltpu.roll(even, half, 1), odd),
    )


def azimuth_kernel(x_ref, inv_hbm, visc_hbm, fwd_hbm, couple_hbm, weight_ref, o_ref,
                   inv_ref, visc_ref, fwd_ref, couple_ref, field_ref, image_ref, sems):
    groups, rows, _ = x_ref.shape
    pairs = (
        (inv_hbm, inv_ref), (visc_hbm, visc_ref), (fwd_hbm, fwd_ref), (couple_hbm, couple_ref),
    )
    copies = [
        pltpu.make_async_copy(source, target, sems.at[k])
        for k, (source, target) in enumerate(pairs)
    ]
    copies[0].start()
    lane = lax.broadcasted_iota(jnp.int32, (rows, LANES), 1)
    low = lane < LANES // 2
    for t in range(groups // 2):
        first, second = swap_halves(
            x_ref[2 * t].astype(jnp.float32), x_ref[2 * t + 1].astype(jnp.float32), low
        )
        field_ref[0, :, t * LANES:(t + 1) * LANES] = first.astype(jnp.bfloat16)
        field_ref[1, :, t * LANES:(t + 1) * LANES] = second.astype(jnp.bfloat16)
        if t in STAGES:
            copies[STAGES.index(t) + 1].start()
    for c in range(2):
        if c == 0:
            copies[0].wait()
        physical = jnp.dot(field_ref[c], inv_ref[...], preferred_element_type=jnp.float32)
        if c == 0:
            copies[1].wait()
        product = (visc_ref[...] * physical).astype(jnp.bfloat16)
        if c == 0:
            copies[2].wait()
        spectral = jnp.dot(
            product, fwd_ref[...], preferred_element_type=jnp.float32
        ).astype(jnp.bfloat16)
        column = lax.broadcasted_iota(jnp.int32, (1, 2 * MODES), 1)
        order = (column // 64) * 32 + column % 32
        scale = 4.0 * (order.astype(jnp.float32) / MODES) ** 2
        if c == 0:
            copies[3].wait()
        image_ref[c] = jnp.dot(
            couple_ref[...], spectral, preferred_element_type=jnp.float32
        ) + (weight_ref[...] * scale) * spectral.astype(jnp.float32)
    for t in range(groups // 2):
        pair = swap_halves(
            image_ref[0, :, t * LANES:(t + 1) * LANES],
            image_ref[1, :, t * LANES:(t + 1) * LANES],
            low,
        )
        for half in range(2):
            merge_axial(o_ref.at[2 * t + half], pair[half], rows // NODE)


def merge_axial(o_ref, image, piece):
    place = lax.broadcasted_iota(jnp.int32, (piece, LANES), 0)
    lowest = []
    for a in range(FACE):
        start = a * FACE * piece
        inner = image[start:start + piece]
        outer = image[start + 8 * piece:start + 9 * piece]
        outer = outer + jnp.where(place < piece - 1, pltpu.roll(inner, piece - 1, 0), 0.0)
        kept = image[start + piece:start + 8 * piece]
        o_ref[a * 8 * piece:(a + 1) * 8 * piece] = jnp.concatenate(
            [kept, outer], axis=0
        ).astype(jnp.bfloat16)
        lowest.append(inner[:1])
    lowest.append(jnp.zeros((EXTRA - FACE, LANES), jnp.float32))
    o_ref[FACE * 8 * piece:] = jnp.concatenate(lowest, axis=0).astype(jnp.bfloat16)


def azimuth(gathered, inverse, viscosity, forward, coupling, weight):
    groups, rows, _ = gathered.shape
    sent = FACE * 8 * (rows // NODE) + EXTRA
    vmem = pl.BlockSpec(memory_space=pltpu.VMEM)
    hbm = pl.BlockSpec(memory_space=pltpu.HBM)
    held = [
        pltpu.with_memory_space_constraint(value, pltpu.HBM)
        for value in (inverse, viscosity, forward, coupling)
    ]
    return pl.pallas_call(
        azimuth_kernel,
        in_specs=[vmem, hbm, hbm, hbm, hbm, vmem],
        out_specs=vmem,
        out_shape=jax.ShapeDtypeStruct((groups, sent, LANES), jnp.bfloat16),
        scratch_shapes=[pltpu.VMEM(value.shape, value.dtype) for value in held] + [
            pltpu.VMEM((2, rows, 2 * MODES), jnp.bfloat16),
            pltpu.VMEM((2, rows, 2 * MODES), jnp.float32),
            pltpu.SemaphoreType.DMA((len(held),)),
        ],
        compiler_params=params(40),
        name="azimuth_product_and_coupling",
    )(gathered, *held, weight)


def lowest_nodes(values):
    groups = values.shape[0]
    return jnp.broadcast_to(
        values[:, None, :], (groups, LANES // groups, LANES)
    ).reshape(LANES, LANES)


def row_of(extra, a):
    place = lax.broadcasted_iota(jnp.int32, extra.shape, 1)
    return jnp.sum(jnp.where(place == a, extra, 0.0), axis=1)


def write_nodes(o_ref, image, lowest):
    groups, rows, _ = image.shape
    piece = rows // 8
    place = lax.broadcasted_iota(jnp.int32, (LANES, LANES), 1) % EZ
    zero = lowest_nodes(lowest).T
    tiles = []
    for b in range(8):
        tiles.append(image[:, b * piece:(b + 1) * piece].reshape(LANES, LANES).T)
    crossing = (place % piece == piece - 1) & (place < EZ - 1)
    tiles[7] = tiles[7] + jnp.where(crossing, pltpu.roll(zero, LANES - 1, 1), 0.0)
    tiles.insert(0, jnp.where(place == 0, zero, pltpu.roll(tiles[7], 1, 1)))
    for b in range(FACE):
        o_ref[:, :, b] = tiles[b].reshape(2, 2, -1, LANES)


def interior_kernel(z_ref, extra_ref, o_ref):
    a = pl.program_id(0) + 1
    write_nodes(
        o_ref,
        z_ref[...].astype(jnp.float32),
        row_of(extra_ref[...].astype(jnp.float32), a),
    )


def face_kernel(odd_ref, inner_ref, outer_ref, extra_ref, near_ref, far_ref, kept_ref, o_ref):
    tail = near_ref.shape[1]
    rows = inner_ref.shape[1]
    odd = odd_ref[0] == 1
    wide = lambda value: value.astype(jnp.float32)
    extra = wide(extra_ref[...])

    @pl.when(pl.program_id(0) == 0)
    def _():
        prev = jnp.where(odd, wide(near_ref[1]), wide(far_ref[1]))
        other = jnp.concatenate([prev[:, :rows], wide(outer_ref[:-tail])], axis=0)
        ends = jnp.concatenate([row_of(prev[:, rows:], 8), row_of(extra[:-tail], 8)], axis=0)
        write_nodes(o_ref, wide(inner_ref[...]) + other, row_of(extra, 0) + ends)

    @pl.when(pl.program_id(0) == 1)
    def _():
        after = jnp.where(odd, wide(far_ref[0]), wide(near_ref[0]))
        other = jnp.concatenate([wide(inner_ref[tail:]), after[:, :rows]], axis=0)
        ends = jnp.concatenate([row_of(extra[tail:], 0), row_of(after[:, rows:], 0)], axis=0)
        write_nodes(o_ref, wide(outer_ref[...]) + other, row_of(extra, 8) + ends)


def assemble(returned, modes, piece):
    groups = returned.shape[0]
    rows = 8 * piece
    faces = EZ // piece
    count = lax.axis_size("elem")
    inner = jnp.concatenate([returned[:faces, :rows], returned[:faces, -EXTRA:]], axis=1)
    outer = jnp.concatenate(
        [returned[-faces:, 8 * rows:9 * rows], returned[-faces:, -EXTRA:]], axis=1
    )
    both = jnp.stack([inner, outer])
    near = lax.ppermute(both, "elem", [(e, e ^ 1) for e in range(count)])
    far = lax.ppermute(both, "elem", [(e, ((e + 1) ^ 1) - 1) for e in range(1, count - 1)])
    odd = (lax.axis_index("elem") % 2).reshape(1)
    out = jax.ShapeDtypeStruct((2, 2, NODE, modes, LANES), jnp.float32)
    block = (groups, rows, LANES)
    extra_block = pl.BlockSpec(
        (groups, EXTRA, LANES), lambda i: (0, FACE * rows // EXTRA, 0)
    )
    image_block = (2, 2, FACE, modes, LANES)
    image = pl.pallas_call(
        interior_kernel,
        grid=(7,),
        in_specs=[pl.BlockSpec(block, lambda i: (0, i + 1, 0)), extra_block],
        out_specs=pl.BlockSpec(image_block, lambda i: (0, 0, i + 1, 0, 0)),
        out_shape=out,
        compiler_params=params(12, "arbitrary"),
        name="interior_nodes",
    )(returned, returned)
    face_block = pl.BlockSpec(both.shape, lambda i: (0, 0, 0, 0))
    return pl.pallas_call(
        face_kernel,
        grid=(2,),
        in_specs=[
            pl.BlockSpec(memory_space=pltpu.SMEM),
            pl.BlockSpec(block, lambda i: (0, 0, 0)),
            pl.BlockSpec(block, lambda i: (0, 8, 0)),
            extra_block,
            face_block,
            face_block,
            pl.BlockSpec(memory_space=pl.ANY),
        ],
        out_specs=pl.BlockSpec(image_block, lambda i: (0, 0, 8 * i, 0, 0)),
        out_shape=out,
        input_output_aliases={6: 0},
        compiler_params=params(12, "arbitrary"),
        name="radial_face_nodes",
    )(odd, returned, returned, returned, near, far, image)


def body(velocity, concentration, stiffness, block_ids, radial_weight):
    modes = velocity.shape[2]
    elements = velocity.shape[4]
    groups = lax.axis_size("mode")
    piece = elements // groups
    rows = NODE * piece
    packed = pack(velocity.transpose(0, 1, 3, 2, 4), groups, piece)
    gathered = lax.all_to_all(
        packed.reshape(groups, rows, LANES), "mode", split_axis=0, concat_axis=0, tiled=True
    )

    inverse, forward = azimuth_tables(groups)
    viscosity = (
        1.0
        - concentration.transpose(1, 2, 0).reshape(rows, NPHI).astype(jnp.float32)
        / packing_limit
    ) ** (-krieger_power)
    first = lax.axis_index("mode") * piece
    ids = lax.dynamic_slice(block_ids, (first,), (piece,))
    weight = lax.dynamic_slice(radial_weight, (0, first), (NODE, piece)).reshape(rows, 1)
    row = jnp.arange(rows, dtype=jnp.int32)
    spread = (row[:, None] // piece == jnp.arange(NODE)[None, :]).astype(jnp.bfloat16)
    ids = jnp.tile(ids, NODE)
    kinds = jnp.einsum("ni,tij->tnj", spread, stiffness, preferred_element_type=jnp.bfloat16)
    chosen = jnp.zeros((rows, NODE), jnp.bfloat16)
    for kind in range(stiffness.shape[0]):
        chosen = jnp.where((ids == kind)[:, None], kinds[kind], chosen)
    coupling = jnp.where(
        row[:, None] % piece == row[None, :] % piece,
        jnp.einsum("nj,mj->nm", chosen, spread, preferred_element_type=jnp.bfloat16),
        jnp.bfloat16(0),
    )

    images = azimuth(gathered, inverse, viscosity, forward, coupling, weight)
    returned = lax.all_to_all(images, "mode", split_axis=0, concat_axis=0, tiled=True)
    image = assemble(returned, modes, piece)
    return image.transpose(0, 1, 3, 2, 4)


def solution(mesh):
    in_specs = (
        P(None, None, "mode", None, "elem"),
        P(None, None, ("elem", "mode")),
        P(),
        P("elem"),
        P(None, "elem"),
    )
    out_specs = P(None, None, "mode", None, "elem")
    return jax.shard_map(body, mesh=mesh, in_specs=in_specs, out_specs=out_specs, check_vma=False)
```

```python
import functools

import jax
import jax.numpy as jnp
from jax import lax
from jax.experimental import pallas as pl
from jax.experimental.pallas import tpu as pltpu
from jax.sharding import PartitionSpec as P

MODES = 512
NPHI = 1024
NODE = 81
EZ = 16
LANES = 128
FACE = 9
EXTRA = 16
PLANES = 256

packing_limit = 0.68
krieger_power = 1.82


def params(mebibytes, *semantics):
    return pltpu.CompilerParams(
        vmem_limit_bytes=mebibytes * 1024 * 1024, dimension_semantics=semantics or None
    )


def azimuth_tables(groups):
    planes = jnp.arange(NPHI, dtype=jnp.int32)
    orders = jnp.arange(MODES, dtype=jnp.int32)
    phase = orders[:, None] * planes[None, :] % NPHI
    angle = 2.0 * jnp.pi / NPHI * phase.astype(jnp.float32)
    shape = (groups, MODES // groups, NPHI)
    base = jnp.stack(
        [
            jnp.cos(angle).astype(jnp.bfloat16).reshape(shape),
            (-jnp.sin(angle)).astype(jnp.bfloat16).reshape(shape),
        ],
        axis=1,
    ).reshape(2 * MODES, NPHI)
    base = lax.optimization_barrier(base)
    column = jnp.arange(2 * MODES, dtype=jnp.int32)
    weight = jnp.where(column % 32 + column // 64 == 0, 1, 2)
    inverse = base * weight.astype(jnp.bfloat16)[:, None]
    forward = base.T / jnp.bfloat16(NPHI)
    return inverse, forward


PACK_STEP = 9


def pack_kernel(v_hbm, o_hbm, v_ref, o_ref, v_sems, o_sems):
    steps = NODE // PACK_STEP
    nodes = [pl.ds(i * PACK_STEP, PACK_STEP) for i in range(steps)]
    arrivals = [
        pltpu.make_async_copy(v_hbm.at[:, :, nodes[i]], v_ref.at[:, :, nodes[i]], v_sems.at[i])
        for i in range(steps)
    ]
    departures = [
        pltpu.make_async_copy(o_ref.at[:, nodes[i]], o_hbm.at[:, nodes[i]], o_sems.at[i])
        for i in range(steps)
    ]
    for copy in arrivals:
        copy.start()
    for i in range(steps):
        arrivals[i].wait()
        for k in range(i * PACK_STEP, (i + 1) * PACK_STEP):
            tile = v_ref[:, :, k].reshape(LANES, LANES)
            o_ref[:, k] = tile.T.reshape(o_ref.shape[0], -1, LANES)
        departures[i].start()
    for copy in departures:
        copy.wait()


def pack(velocity, groups, piece):
    steps = NODE // PACK_STEP
    hbm = pl.BlockSpec(memory_space=pltpu.HBM)
    packed = (groups, NODE, piece, LANES)
    return pl.pallas_call(
        pack_kernel,
        in_specs=[hbm],
        out_specs=hbm,
        out_shape=jax.ShapeDtypeStruct(packed, jnp.bfloat16),
        scratch_shapes=[
            pltpu.VMEM(velocity.shape, jnp.bfloat16),
            pltpu.VMEM(packed, jnp.bfloat16),
            pltpu.SemaphoreType.DMA((steps,)),
            pltpu.SemaphoreType.DMA((steps,)),
        ],
        compiler_params=params(58),
        name="pack_by_element_group",
    )(pltpu.with_memory_space_constraint(velocity, pltpu.HBM))


def swap_halves(even, odd, low):
    half = LANES // 2
    return (
        jnp.where(low, even, pltpu.roll(odd, half, 1)),
        jnp.where(low, pltpu.roll(even, half, 1), odd),
    )


def azimuth_kernel(x_ref, inv_hbm, visc_hbm, fwd_hbm, couple_hbm, weight_ref, o_ref,
                   inv_ref, visc_ref, fwd_ref, couple_ref, field_ref, product_ref, image_ref,
                   sems):
    groups, rows, _ = x_ref.shape
    parts = NPHI // PLANES
    planes = [slice(q * PLANES, (q + 1) * PLANES) for q in range(parts)]

    def copy_of(source, target, place):
        return pltpu.make_async_copy(source, target, sems.at[place])

    tables = [
        (
            copy_of(inv_hbm.at[:, planes[q]], inv_ref.at[:, planes[q]], 2 * q),
            copy_of(visc_hbm.at[:, planes[q]], visc_ref.at[:, planes[q]], 2 * q + 1),
        )
        for q in range(parts)
    ]
    forward = copy_of(fwd_hbm, fwd_ref, 2 * parts)
    coupling = copy_of(couple_hbm, couple_ref, 2 * parts + 1)
    for part in tables:
        for copy in part:
            copy.start()
    forward.start()
    coupling.start()
    lane = lax.broadcasted_iota(jnp.int32, (rows, LANES), 1)
    low = lane < LANES // 2

    def gather_field(c):
        for t in range(groups // 2):
            pair = swap_halves(
                x_ref[2 * t].astype(jnp.float32), x_ref[2 * t + 1].astype(jnp.float32), low
            )
            field_ref[c, :, t * LANES:(t + 1) * LANES] = pair[c].astype(jnp.bfloat16)

    gather_field(0)
    for q in range(parts):
        for copy in tables[q]:
            copy.wait()
        for c in range(2):
            if q == 0 and c == 1:
                gather_field(1)
            physical = jnp.dot(
                field_ref[c], inv_ref[:, planes[q]], preferred_element_type=jnp.float32
            )
            product_ref[c, :, planes[q]] = (visc_ref[:, planes[q]] * physical).astype(
                jnp.bfloat16
            )
    forward.wait()
    coupling.wait()
    column = lax.broadcasted_iota(jnp.int32, (1, 2 * MODES), 1)
    order = (column // 64) * 32 + column % 32
    scale = 4.0 * (order.astype(jnp.float32) / MODES) ** 2
    for c in range(2):
        spectral = jnp.dot(
            product_ref[c], fwd_ref[...], preferred_element_type=jnp.float32
        ).astype(jnp.bfloat16)
        image_ref[c] = jnp.dot(
            couple_ref[...], spectral, preferred_element_type=jnp.float32
        ) + (weight_ref[...] * scale) * spectral.astype(jnp.float32)
    for t in range(groups // 2):
        pair = swap_halves(
            image_ref[0, :, t * LANES:(t + 1) * LANES],
            image_ref[1, :, t * LANES:(t + 1) * LANES],
            low,
        )
        for half in range(2):
            merge_axial(o_ref.at[2 * t + half], pair[half], rows // NODE)


def merge_axial(o_ref, image, piece):
    place = lax.broadcasted_iota(jnp.int32, (piece, LANES), 0)
    lowest = []
    for a in range(FACE):
        start = a * FACE * piece
        inner = image[start:start + piece]
        outer = image[start + 8 * piece:start + 9 * piece]
        outer = outer + jnp.where(place < piece - 1, pltpu.roll(inner, piece - 1, 0), 0.0)
        kept = image[start + piece:start + 8 * piece]
        o_ref[a * 8 * piece:(a + 1) * 8 * piece] = jnp.concatenate(
            [kept, outer], axis=0
        ).astype(jnp.bfloat16)
        lowest.append(inner[:1])
    lowest.append(jnp.zeros((EXTRA - FACE, LANES), jnp.float32))
    o_ref[FACE * 8 * piece:] = jnp.concatenate(lowest, axis=0).astype(jnp.bfloat16)


def azimuth(gathered, inverse, viscosity, forward, coupling, weight):
    groups, rows, _ = gathered.shape
    sent = FACE * 8 * (rows // NODE) + EXTRA
    vmem = pl.BlockSpec(memory_space=pltpu.VMEM)
    hbm = pl.BlockSpec(memory_space=pltpu.HBM)
    held = [
        pltpu.with_memory_space_constraint(value, pltpu.HBM)
        for value in (inverse, viscosity, forward, coupling)
    ]
    return pl.pallas_call(
        azimuth_kernel,
        in_specs=[vmem, hbm, hbm, hbm, hbm, vmem],
        out_specs=vmem,
        out_shape=jax.ShapeDtypeStruct((groups, sent, LANES), jnp.bfloat16),
        scratch_shapes=[pltpu.VMEM(value.shape, value.dtype) for value in held] + [
            pltpu.VMEM((2, rows, 2 * MODES), jnp.bfloat16),
            pltpu.VMEM((2, rows, NPHI), jnp.bfloat16),
            pltpu.VMEM((2, rows, 2 * MODES), jnp.float32),
            pltpu.SemaphoreType.DMA((2 * (NPHI // PLANES) + 2,)),
        ],
        compiler_params=params(40),
        name="azimuth_product_and_coupling",
    )(gathered, *held, weight)


def lowest_nodes(values):
    groups = values.shape[0]
    return jnp.broadcast_to(
        values[:, None, :], (groups, LANES // groups, LANES)
    ).reshape(LANES, LANES)


def row_of(extra, a):
    place = lax.broadcasted_iota(jnp.int32, extra.shape, 1)
    return jnp.sum(jnp.where(place == a, extra, 0.0), axis=1)


def write_nodes(o_ref, image, lowest):
    groups, rows, _ = image.shape
    piece = rows // 8
    place = lax.broadcasted_iota(jnp.int32, (LANES, LANES), 1) % EZ
    zero = lowest_nodes(lowest).T
    tiles = []
    for b in range(8):
        tiles.append(image[:, b * piece:(b + 1) * piece].reshape(LANES, LANES).T)
    crossing = (place % piece == piece - 1) & (place < EZ - 1)
    tiles[7] = tiles[7] + jnp.where(crossing, pltpu.roll(zero, LANES - 1, 1), 0.0)
    tiles.insert(0, jnp.where(place == 0, zero, pltpu.roll(tiles[7], 1, 1)))
    for b in range(FACE):
        o_ref[:, :, b] = tiles[b].reshape(2, 2, -1, LANES)


def interior_kernel(z_ref, extra_ref, o_ref):
    a = pl.program_id(0) + 1
    write_nodes(
        o_ref,
        z_ref[...].astype(jnp.float32),
        row_of(extra_ref[...].astype(jnp.float32), a),
    )


def face_kernel(odd_ref, inner_ref, outer_ref, extra_ref, near_ref, far_ref, kept_ref, o_ref):
    tail = near_ref.shape[1]
    rows = inner_ref.shape[1]
    odd = odd_ref[0] == 1
    wide = lambda value: value.astype(jnp.float32)
    extra = wide(extra_ref[...])

    @pl.when(pl.program_id(0) == 0)
    def _():
        prev = jnp.where(odd, wide(near_ref[1]), wide(far_ref[1]))
        other = jnp.concatenate([prev[:, :rows], wide(outer_ref[:-tail])], axis=0)
        ends = jnp.concatenate([row_of(prev[:, rows:], 8), row_of(extra[:-tail], 8)], axis=0)
        write_nodes(o_ref, wide(inner_ref[...]) + other, row_of(extra, 0) + ends)

    @pl.when(pl.program_id(0) == 1)
    def _():
        after = jnp.where(odd, wide(far_ref[0]), wide(near_ref[0]))
        other = jnp.concatenate([wide(inner_ref[tail:]), after[:, :rows]], axis=0)
        ends = jnp.concatenate([row_of(extra[tail:], 0), row_of(after[:, rows:], 0)], axis=0)
        write_nodes(o_ref, wide(outer_ref[...]) + other, row_of(extra, 8) + ends)


def assemble(returned, modes, piece):
    groups = returned.shape[0]
    rows = 8 * piece
    faces = EZ // piece
    count = lax.axis_size("elem")
    inner = jnp.concatenate([returned[:faces, :rows], returned[:faces, -EXTRA:]], axis=1)
    outer = jnp.concatenate(
        [returned[-faces:, 8 * rows:9 * rows], returned[-faces:, -EXTRA:]], axis=1
    )
    both = jnp.stack([inner, outer])
    near = lax.ppermute(both, "elem", [(e, e ^ 1) for e in range(count)])
    far = lax.ppermute(both, "elem", [(e, ((e + 1) ^ 1) - 1) for e in range(1, count - 1)])
    odd = (lax.axis_index("elem") % 2).reshape(1)
    out = jax.ShapeDtypeStruct((2, 2, NODE, modes, LANES), jnp.float32)
    block = (groups, rows, LANES)
    extra_block = pl.BlockSpec(
        (groups, EXTRA, LANES), lambda i: (0, FACE * rows // EXTRA, 0)
    )
    image_block = (2, 2, FACE, modes, LANES)
    image = pl.pallas_call(
        interior_kernel,
        grid=(7,),
        in_specs=[pl.BlockSpec(block, lambda i: (0, i + 1, 0)), extra_block],
        out_specs=pl.BlockSpec(image_block, lambda i: (0, 0, i + 1, 0, 0)),
        out_shape=out,
        compiler_params=params(12, "arbitrary"),
        name="interior_nodes",
    )(returned, returned)
    face_block = pl.BlockSpec(both.shape, lambda i: (0, 0, 0, 0))
    return pl.pallas_call(
        face_kernel,
        grid=(2,),
        in_specs=[
            pl.BlockSpec(memory_space=pltpu.SMEM),
            pl.BlockSpec(block, lambda i: (0, 0, 0)),
            pl.BlockSpec(block, lambda i: (0, 8, 0)),
            extra_block,
            face_block,
            face_block,
            pl.BlockSpec(memory_space=pl.ANY),
        ],
        out_specs=pl.BlockSpec(image_block, lambda i: (0, 0, 8 * i, 0, 0)),
        out_shape=out,
        input_output_aliases={6: 0},
        compiler_params=params(12, "arbitrary"),
        name="radial_face_nodes",
    )(odd, returned, returned, returned, near, far, image)


def body(velocity, concentration, stiffness, block_ids, radial_weight):
    modes = velocity.shape[2]
    elements = velocity.shape[4]
    groups = lax.axis_size("mode")
    piece = elements // groups
    rows = NODE * piece
    packed = pack(velocity.transpose(0, 1, 3, 2, 4), groups, piece)
    gathered = lax.all_to_all(
        packed.reshape(groups, rows, LANES), "mode", split_axis=0, concat_axis=0, tiled=True
    )

    inverse, forward = azimuth_tables(groups)
    viscosity = (
        1.0
        - concentration.transpose(1, 2, 0).reshape(rows, NPHI).astype(jnp.float32)
        / packing_limit
    ) ** (-krieger_power)
    first = lax.axis_index("mode") * piece
    ids = lax.dynamic_slice(block_ids, (first,), (piece,))
    weight = lax.dynamic_slice(radial_weight, (0, first), (NODE, piece)).reshape(rows, 1)
    row = jnp.arange(rows, dtype=jnp.int32)
    spread = (row[:, None] // piece == jnp.arange(NODE)[None, :]).astype(jnp.bfloat16)
    ids = jnp.tile(ids, NODE)
    kinds = jnp.einsum("ni,tij->tnj", spread, stiffness, preferred_element_type=jnp.bfloat16)
    chosen = jnp.zeros((rows, NODE), jnp.bfloat16)
    for kind in range(stiffness.shape[0]):
        chosen = jnp.where((ids == kind)[:, None], kinds[kind], chosen)
    coupling = jnp.where(
        row[:, None] % piece == row[None, :] % piece,
        jnp.einsum("nj,mj->nm", chosen, spread, preferred_element_type=jnp.bfloat16),
        jnp.bfloat16(0),
    )

    images = azimuth(gathered, inverse, viscosity, forward, coupling, weight)
    returned = lax.all_to_all(images, "mode", split_axis=0, concat_axis=0, tiled=True)
    image = assemble(returned, modes, piece)
    return image.transpose(0, 1, 3, 2, 4)


def solution(mesh):
    in_specs = (
        P(None, None, "mode", None, "elem"),
        P(None, None, ("elem", "mode")),
        P(),
        P("elem"),
        P(None, "elem"),
    )
    out_specs = P(None, None, "mode", None, "elem")
    return jax.shard_map(body, mesh=mesh, in_specs=in_specs, out_specs=out_specs, check_vma=False)
```

```python
import functools

import jax
import jax.numpy as jnp
from jax import lax
from jax.experimental import pallas as pl
from jax.experimental.pallas import tpu as pltpu
from jax.sharding import PartitionSpec as P

MODES = 512
NPHI = 1024
NODE = 81
EZ = 16
LANES = 128
FACE = 9
EXTRA = 16
PLANES = 256

packing_limit = 0.68
krieger_power = 1.82


def params(mebibytes, *semantics):
    return pltpu.CompilerParams(
        vmem_limit_bytes=mebibytes * 1024 * 1024, dimension_semantics=semantics or None
    )


def azimuth_tables(groups):
    planes = jnp.arange(NPHI, dtype=jnp.int32)
    orders = jnp.arange(MODES, dtype=jnp.int32)
    phase = orders[:, None] * planes[None, :] % NPHI
    angle = 2.0 * jnp.pi / NPHI * phase.astype(jnp.float32)
    shape = (groups, MODES // groups, NPHI)
    base = jnp.stack(
        [
            jnp.cos(angle).astype(jnp.bfloat16).reshape(shape),
            (-jnp.sin(angle)).astype(jnp.bfloat16).reshape(shape),
        ],
        axis=1,
    ).reshape(2 * MODES, NPHI)
    base = lax.optimization_barrier(base)
    column = jnp.arange(2 * MODES, dtype=jnp.int32)
    weight = jnp.where(column % 32 + column // 64 == 0, 1, 2)
    inverse = base * weight.astype(jnp.bfloat16)[:, None]
    forward = base.T / jnp.bfloat16(NPHI)
    return inverse, forward


PACK_STEP = 9


def pack_kernel(v_hbm, o_hbm, v_ref, o_ref, v_sems, o_sems):
    steps = NODE // PACK_STEP
    nodes = [pl.ds(i * PACK_STEP, PACK_STEP) for i in range(steps)]
    arrivals = [
        pltpu.make_async_copy(v_hbm.at[:, :, nodes[i]], v_ref.at[:, :, nodes[i]], v_sems.at[i])
        for i in range(steps)
    ]
    departures = [
        pltpu.make_async_copy(o_ref.at[:, nodes[i]], o_hbm.at[:, nodes[i]], o_sems.at[i])
        for i in range(steps)
    ]
    for copy in arrivals:
        copy.start()
    for i in range(steps):
        arrivals[i].wait()
        for k in range(i * PACK_STEP, (i + 1) * PACK_STEP):
            tile = v_ref[:, :, k].reshape(LANES, LANES)
            o_ref[:, k] = tile.T.reshape(o_ref.shape[0], -1, LANES)
        departures[i].start()
    for copy in departures:
        copy.wait()


def pack(velocity, groups, piece):
    steps = NODE // PACK_STEP
    hbm = pl.BlockSpec(memory_space=pltpu.HBM)
    packed = (groups, NODE, piece, LANES)
    return pl.pallas_call(
        pack_kernel,
        in_specs=[hbm],
        out_specs=hbm,
        out_shape=jax.ShapeDtypeStruct(packed, jnp.bfloat16),
        scratch_shapes=[
            pltpu.VMEM(velocity.shape, jnp.bfloat16),
            pltpu.VMEM(packed, jnp.bfloat16),
            pltpu.SemaphoreType.DMA((steps,)),
            pltpu.SemaphoreType.DMA((steps,)),
        ],
        compiler_params=params(58),
        name="pack_by_element_group",
    )(pltpu.with_memory_space_constraint(velocity, pltpu.HBM))


def swap_halves(even, odd, low):
    half = LANES // 2
    return (
        jnp.where(low, even, pltpu.roll(odd, half, 1)),
        jnp.where(low, pltpu.roll(even, half, 1), odd),
    )


def azimuth_kernel(x_ref, inv_hbm, visc_hbm, fwd_hbm, couple_hbm, weight_ref, o_ref,
                   inv_ref, visc_ref, fwd_ref, couple_ref, field_ref, product_ref, sems):
    groups, rows, _ = x_ref.shape
    parts = NPHI // PLANES
    planes = [slice(q * PLANES, (q + 1) * PLANES) for q in range(parts)]

    def copy_of(source, target, place):
        return pltpu.make_async_copy(source, target, sems.at[place])

    tables = [
        (
            copy_of(inv_hbm.at[:, planes[q]], inv_ref.at[:, planes[q]], 2 * q),
            copy_of(visc_hbm.at[:, planes[q]], visc_ref.at[:, planes[q]], 2 * q + 1),
        )
        for q in range(parts)
    ]
    forward = copy_of(fwd_hbm, fwd_ref, 2 * parts)
    coupling = copy_of(couple_hbm, couple_ref, 2 * parts + 1)
    for part in tables:
        for copy in part:
            copy.start()
    forward.start()
    coupling.start()
    lane = lax.broadcasted_iota(jnp.int32, (rows, LANES), 1)
    low = lane < LANES // 2

    def gather_field(c):
        for t in range(groups // 2):
            pair = swap_halves(
                x_ref[2 * t].astype(jnp.float32), x_ref[2 * t + 1].astype(jnp.float32), low
            )
            field_ref[c, :, t * LANES:(t + 1) * LANES] = pair[c].astype(jnp.bfloat16)

    gather_field(0)
    for q in range(parts):
        for copy in tables[q]:
            copy.wait()
        for c in range(2):
            if q == 0 and c == 1:
                gather_field(1)
            physical = jnp.dot(
                field_ref[c], inv_ref[:, planes[q]], preferred_element_type=jnp.float32
            )
            product_ref[c, :, planes[q]] = (visc_ref[:, planes[q]] * physical).astype(
                jnp.bfloat16
            )
    forward.wait()
    coupling.wait()
    column = lax.broadcasted_iota(jnp.int32, (1, 2 * MODES), 1)
    order = (column // 64) * 32 + column % 32
    scale = 4.0 * (order.astype(jnp.float32) / MODES) ** 2
    for c in range(2):
        field_ref[c] = jnp.dot(
            product_ref[c], fwd_ref[...], preferred_element_type=jnp.float32
        ).astype(jnp.bfloat16)
    wide = 2 * LANES
    for n in range(2 * MODES // wide):
        columns = slice(n * wide, (n + 1) * wide)
        images = []
        for c in range(2):
            spectral = field_ref[c, :, columns]
            images.append(
                jnp.dot(couple_ref[...], spectral, preferred_element_type=jnp.float32)
                + (weight_ref[...] * scale[:, columns]) * spectral.astype(jnp.float32)
            )
        for t in range(2):
            pair = swap_halves(
                images[0][:, t * LANES:(t + 1) * LANES],
                images[1][:, t * LANES:(t + 1) * LANES],
                low,
            )
            for half in range(2):
                merge_axial(o_ref.at[4 * n + 2 * t + half], pair[half], rows // NODE)


def merge_axial(o_ref, image, piece):
    place = lax.broadcasted_iota(jnp.int32, (piece, LANES), 0)
    lowest = []
    for a in range(FACE):
        start = a * FACE * piece
        inner = image[start:start + piece]
        outer = image[start + 8 * piece:start + 9 * piece]
        outer = outer + jnp.where(place < piece - 1, pltpu.roll(inner, piece - 1, 0), 0.0)
        kept = image[start + piece:start + 8 * piece]
        o_ref[a * 8 * piece:(a + 1) * 8 * piece] = jnp.concatenate(
            [kept, outer], axis=0
        ).astype(jnp.bfloat16)
        lowest.append(inner[:1])
    lowest.append(jnp.zeros((EXTRA - FACE, LANES), jnp.float32))
    o_ref[FACE * 8 * piece:] = jnp.concatenate(lowest, axis=0).astype(jnp.bfloat16)


def azimuth(gathered, inverse, viscosity, forward, coupling, weight):
    groups, rows, _ = gathered.shape
    sent = FACE * 8 * (rows // NODE) + EXTRA
    vmem = pl.BlockSpec(memory_space=pltpu.VMEM)
    hbm = pl.BlockSpec(memory_space=pltpu.HBM)
    held = [
        pltpu.with_memory_space_constraint(value, pltpu.HBM)
        for value in (inverse, viscosity, forward, coupling)
    ]
    return pl.pallas_call(
        azimuth_kernel,
        in_specs=[vmem, hbm, hbm, hbm, hbm, vmem],
        out_specs=vmem,
        out_shape=jax.ShapeDtypeStruct((groups, sent, LANES), jnp.bfloat16),
        scratch_shapes=[pltpu.VMEM(value.shape, value.dtype) for value in held] + [
            pltpu.VMEM((2, rows, 2 * MODES), jnp.bfloat16),
            pltpu.VMEM((2, rows, NPHI), jnp.bfloat16),
            pltpu.SemaphoreType.DMA((2 * (NPHI // PLANES) + 2,)),
        ],
        compiler_params=params(40),
        name="azimuth_product_and_coupling",
    )(gathered, *held, weight)


def lowest_nodes(values):
    groups = values.shape[0]
    return jnp.broadcast_to(
        values[:, None, :], (groups, LANES // groups, LANES)
    ).reshape(LANES, LANES)


def row_of(extra, a):
    place = lax.broadcasted_iota(jnp.int32, extra.shape, 1)
    return jnp.sum(jnp.where(place == a, extra, 0.0), axis=1)


def write_nodes(o_ref, image, lowest):
    groups, rows, _ = image.shape
    piece = rows // 8
    place = lax.broadcasted_iota(jnp.int32, (LANES, LANES), 1) % EZ
    zero = lowest_nodes(lowest).T
    tiles = []
    for b in range(8):
        tiles.append(image[:, b * piece:(b + 1) * piece].reshape(LANES, LANES).T)
    crossing = (place % piece == piece - 1) & (place < EZ - 1)
    tiles[7] = tiles[7] + jnp.where(crossing, pltpu.roll(zero, LANES - 1, 1), 0.0)
    tiles.insert(0, jnp.where(place == 0, zero, pltpu.roll(tiles[7], 1, 1)))
    for b in range(FACE):
        o_ref[:, :, b] = tiles[b].reshape(2, 2, -1, LANES)


def interior_kernel(z_ref, extra_ref, o_ref):
    a = pl.program_id(0) + 1
    write_nodes(
        o_ref,
        z_ref[...].astype(jnp.float32),
        row_of(extra_ref[...].astype(jnp.float32), a),
    )


def face_kernel(odd_ref, inner_ref, outer_ref, extra_ref, near_ref, far_ref, kept_ref, o_ref):
    tail = near_ref.shape[1]
    rows = inner_ref.shape[1]
    odd = odd_ref[0] == 1
    wide = lambda value: value.astype(jnp.float32)
    extra = wide(extra_ref[...])

    @pl.when(pl.program_id(0) == 0)
    def _():
        prev = jnp.where(odd, wide(near_ref[1]), wide(far_ref[1]))
        other = jnp.concatenate([prev[:, :rows], wide(outer_ref[:-tail])], axis=0)
        ends = jnp.concatenate([row_of(prev[:, rows:], 8), row_of(extra[:-tail], 8)], axis=0)
        write_nodes(o_ref, wide(inner_ref[...]) + other, row_of(extra, 0) + ends)

    @pl.when(pl.program_id(0) == 1)
    def _():
        after = jnp.where(odd, wide(far_ref[0]), wide(near_ref[0]))
        other = jnp.concatenate([wide(inner_ref[tail:]), after[:, :rows]], axis=0)
        ends = jnp.concatenate([row_of(extra[tail:], 0), row_of(after[:, rows:], 0)], axis=0)
        write_nodes(o_ref, wide(outer_ref[...]) + other, row_of(extra, 8) + ends)


def assemble(returned, modes, piece):
    groups = returned.shape[0]
    rows = 8 * piece
    faces = EZ // piece
    count = lax.axis_size("elem")
    inner = jnp.concatenate([returned[:faces, :rows], returned[:faces, -EXTRA:]], axis=1)
    outer = jnp.concatenate(
        [returned[-faces:, 8 * rows:9 * rows], returned[-faces:, -EXTRA:]], axis=1
    )
    both = jnp.stack([inner, outer])
    near = lax.ppermute(both, "elem", [(e, e ^ 1) for e in range(count)])
    far = lax.ppermute(both, "elem", [(e, ((e + 1) ^ 1) - 1) for e in range(1, count - 1)])
    odd = (lax.axis_index("elem") % 2).reshape(1)
    out = jax.ShapeDtypeStruct((2, 2, NODE, modes, LANES), jnp.float32)
    block = (groups, rows, LANES)
    extra_block = pl.BlockSpec(
        (groups, EXTRA, LANES), lambda i: (0, FACE * rows // EXTRA, 0)
    )
    image_block = (2, 2, FACE, modes, LANES)
    image = pl.pallas_call(
        interior_kernel,
        grid=(7,),
        in_specs=[pl.BlockSpec(block, lambda i: (0, i + 1, 0)), extra_block],
        out_specs=pl.BlockSpec(image_block, lambda i: (0, 0, i + 1, 0, 0)),
        out_shape=out,
        compiler_params=params(12, "arbitrary"),
        name="interior_nodes",
    )(returned, returned)
    face_block = pl.BlockSpec(both.shape, lambda i: (0, 0, 0, 0))
    return pl.pallas_call(
        face_kernel,
        grid=(2,),
        in_specs=[
            pl.BlockSpec(memory_space=pltpu.SMEM),
            pl.BlockSpec(block, lambda i: (0, 0, 0)),
            pl.BlockSpec(block, lambda i: (0, 8, 0)),
            extra_block,
            face_block,
            face_block,
            pl.BlockSpec(memory_space=pl.ANY),
        ],
        out_specs=pl.BlockSpec(image_block, lambda i: (0, 0, 8 * i, 0, 0)),
        out_shape=out,
        input_output_aliases={6: 0},
        compiler_params=params(12, "arbitrary"),
        name="radial_face_nodes",
    )(odd, returned, returned, returned, near, far, image)


def body(velocity, concentration, stiffness, block_ids, radial_weight):
    modes = velocity.shape[2]
    elements = velocity.shape[4]
    groups = lax.axis_size("mode")
    piece = elements // groups
    rows = NODE * piece
    packed = pack(velocity.transpose(0, 1, 3, 2, 4), groups, piece)
    gathered = lax.all_to_all(
        packed.reshape(groups, rows, LANES), "mode", split_axis=0, concat_axis=0, tiled=True
    )

    inverse, forward = azimuth_tables(groups)
    viscosity = (
        1.0
        - concentration.transpose(1, 2, 0).reshape(rows, NPHI).astype(jnp.float32)
        / packing_limit
    ) ** (-krieger_power)
    first = lax.axis_index("mode") * piece
    ids = lax.dynamic_slice(block_ids, (first,), (piece,))
    weight = lax.dynamic_slice(radial_weight, (0, first), (NODE, piece)).reshape(rows, 1)
    row = jnp.arange(rows, dtype=jnp.int32)
    spread = (row[:, None] // piece == jnp.arange(NODE)[None, :]).astype(jnp.bfloat16)
    ids = jnp.tile(ids, NODE)
    kinds = jnp.einsum("ni,tij->tnj", spread, stiffness, preferred_element_type=jnp.bfloat16)
    chosen = jnp.zeros((rows, NODE), jnp.bfloat16)
    for kind in range(stiffness.shape[0]):
        chosen = jnp.where((ids == kind)[:, None], kinds[kind], chosen)
    coupling = jnp.where(
        row[:, None] % piece == row[None, :] % piece,
        jnp.einsum("nj,mj->nm", chosen, spread, preferred_element_type=jnp.bfloat16),
        jnp.bfloat16(0),
    )

    images = azimuth(gathered, inverse, viscosity, forward, coupling, weight)
    returned = lax.all_to_all(images, "mode", split_axis=0, concat_axis=0, tiled=True)
    image = assemble(returned, modes, piece)
    return image.transpose(0, 1, 3, 2, 4)


def solution(mesh):
    in_specs = (
        P(None, None, "mode", None, "elem"),
        P(None, None, ("elem", "mode")),
        P(),
        P("elem"),
        P(None, "elem"),
    )
    out_specs = P(None, None, "mode", None, "elem")
    return jax.shard_map(body, mesh=mesh, in_specs=in_specs, out_specs=out_specs, check_vma=False)
```
